1024 devices in a mesh: section: 16 (over y_hi, x), dp: 64 (over y_lo, z, core).
Axes of the slice: x: 4, y: 8 (y_hi: 4, y_lo: 2; y = y_hi * 2 + y_lo), z: 16, core: 2. Of those that a mesh axis runs over, the one named last changes fastest.
Arguments:
- counts: int32 [16], replicated, may hold values from 1 to 3, 32 in all
- activations: bfloat16 [16, 3, 8192, 1792], P('section', None, 'dp'), may hold values from -16 to 16
- cotangents: bfloat16 [16, 3, 8192, 64], P('section', None, 'dp'), may hold values from -1 to 1
Outputs:
- clipped: float32 [32, 1792, 64], P('section', 'dp')
The draws below stay inside these ranges and needn't reach their ends.
Inputs may be any that keep to these rules, and one draw needn't show every extreme that they name: The counts sum to 32; the largest is 3.
All inputs are finite; a program needn't handle non-finite values.
Results may differ from the reference program's by a relative error of at most 0.003.
Values sent between devices are 32-bit elements; how exact they have to be, the bound alone decides.
No kernel may reach another device: no remote copies, remote signals or barrier semaphores. Data moves between devices by JAX's collectives and lax.ppermute only.
A program may use at most 32 MiB of HBM per device.

```python
import math
import jax
import jax.numpy as jnp
import numpy as np
from jax import lax

D = 1792
RANK = 64
CMAX = 3
TOK = 128
TOKENS = 8192
NDEPTH = 32
N_SECTION = 16


def token_signs(key):
    sign_key = jax.random.fold_in(key, 101)
    flips = jax.random.bernoulli(sign_key, 0.5, (N_SECTION, CMAX, TOKENS, 1))
    return jnp.where(flips, 1.0, -1.0).astype(jnp.float32)


def draw_activations(key, part):
    signs = token_signs(key)
    key = jax.random.fold_in(key, 7)
    noise_key, pattern_key, order_key = jax.random.split(key, 3)
    shape = (N_SECTION, CMAX, TOKENS, D)
    noise = jnp.clip(jax.random.normal(noise_key, shape, jnp.float32), -6.0, 6.0)
    strength = 0.5
    pattern = jnp.clip(jax.random.normal(pattern_key, (N_SECTION, CMAX, 1, D), jnp.float32), -4.0, 4.0)
    replicas = TOKENS // TOK
    order = jax.random.permutation(order_key, replicas)
    owner = order[jnp.arange(TOKENS, dtype=jnp.int32) // TOK]
    block = jnp.arange(D, dtype=jnp.int32) // (D // replicas)
    boost = jnp.where(owner[:, None] == block[None, :], 4.0, 1.0).astype(jnp.float32)
    values = noise * boost + strength * signs * pattern
    return jnp.clip(values, -16.0, 16.0).astype(jnp.bfloat16)


def draw_cotangents(key, part):
    signs = token_signs(key)
    key = jax.random.fold_in(key, 11)
    noise_key, pattern_key = jax.random.split(key, 2)
    shape = (N_SECTION, CMAX, TOKENS, RANK)
    noise = jnp.clip(jax.random.normal(noise_key, shape, jnp.float32), -6.0, 6.0)
    strength = 3.0
    pattern = jnp.clip(jax.random.normal(pattern_key, (N_SECTION, CMAX, 1, RANK), jnp.float32), -4.0, 4.0)
    values = noise * float(TOKENS) ** (-0.5) + strength * signs * pattern / float(TOKENS)
    return jnp.clip(values, -1.0, 1.0).astype(jnp.bfloat16)


def split_up(amount, total, bound, skew):
    portions = [(1 << 20) // math.isqrt(rank ** skew) + 1 for rank in range(2, amount + 1)]
    surplus, holding = total - bound - (amount - 1), [1] * (amount - 1)
    while surplus > 0:
        candidates = [i for i in range(amount - 1) if holding[i] < bound]
        mass, remaining = sum([portions[i] for i in candidates]), surplus
        for i in candidates:
            more = min(bound - holding[i], max(1, remaining * portions[i] // mass), surplus)
            holding[i] = holding[i] + more
            surplus = surplus - more
    return np.array([bound] + holding)


def uneven_parts(stream_key, number_of, total, bound, slope):
    if number_of == 2:
        one = jax.random.randint(stream_key, (), max(1, total - bound), min(bound, total - 1) + 1)
        return jnp.stack([one, total - one])
    tallies = jnp.asarray(split_up(number_of, total, bound, slope), jnp.int32)
    couples = (number_of - 1) // 2
    donor, taker = tallies[1:1 + 2 * couples:2], tallies[2:2 + 2 * couples:2]
    margin = jnp.minimum(donor - 1, bound - taker)
    shifted = jax.random.randint(jax.random.fold_in(stream_key, 1), (couples,), 0, 1 << 20) % (margin + 1)
    tallies = tallies.at[1:1 + 2 * couples:2].set(donor - shifted).at[2:2 + 2 * couples:2].set(taker + shifted)
    return tallies[jax.random.permutation(jax.random.fold_in(stream_key, 2), number_of)]


def setup_inputs(seed: int = 0) -> dict:
    streams_of = jax.random.split(jax.random.key(seed), 4)
    counts = uneven_parts(streams_of[0], N_SECTION, NDEPTH, CMAX, 2).astype(jnp.int32)
    activations = draw_activations(jax.random.fold_in(streams_of[3], 71), 0)
    cotangents = draw_cotangents(jax.random.fold_in(streams_of[3], 71), 0)
    return {"counts": counts, "activations": activations, "cotangents": cotangents}


def reference(counts, activations, cotangents):
    number_of_sections = activations.shape[0]
    number_of_slots = activations.shape[1]

    def section_terms(section_index):
        inputs_here = activations[section_index]
        local_cotangent = cotangents[section_index]
        return jnp.stack([jnp.dot(inputs_here[slot_index].T, local_cotangent[slot_index], preferred_element_type=jnp.float32) for slot_index in range(number_of_slots)])
    partials = lax.map(section_terms, jnp.arange(number_of_sections, dtype=jnp.int32))
    offsets = jnp.cumsum(counts).astype(jnp.int32) - counts
    slot_ids = jnp.arange(number_of_slots, dtype=jnp.int32)
    depth_ids = (offsets[:, None] + slot_ids[None, :] + NDEPTH // 2) % NDEPTH
    valid_slot = slot_ids[None, :] < counts[:, None]
    all_depths = jnp.arange(NDEPTH, dtype=jnp.int32)
    selector = ((depth_ids[:, :, None] == all_depths[None, None, :]) & valid_slot[:, :, None]).astype(jnp.float32)
    gradients = jnp.einsum('ske,skdr->edr', selector, partials, precision=lax.Precision.HIGHEST)
    mean_square = jnp.mean(gradients * gradients)
    factor = jnp.minimum(1.0, 0.5 / jnp.sqrt(mean_square + 1e-06))
    return gradients * factor
```

```python
import functools

import jax
import jax.numpy as jnp
from jax import lax
from jax.experimental import pallas as pl
from jax.experimental.pallas import tpu as pltpu
from jax.sharding import Mesh, PartitionSpec as P

DEPTHS_PER_OWNER = 2
Y_PAIR = 2
CORES = 2
LANES = 128
PAD_ROWS = 16
VMEM = pl.BlockSpec(memory_space=pltpu.VMEM)
SMEM = pl.BlockSpec(memory_space=pltpu.SMEM)


def call(body, shapes, in_specs, scratch=()):
    return pl.pallas_call(
        body,
        out_shape=tuple(jax.ShapeDtypeStruct(s, jnp.float32) for s in shapes),
        in_specs=in_specs,
        out_specs=tuple(VMEM for _ in shapes),
        scratch_shapes=list(scratch),
        compiler_params=pltpu.CompilerParams(vmem_limit_bytes=24 * 1024 * 1024),
    )


def partial_kernel(slots, tokens, rank, chunk, place, a_ref, c_ref, keep_ref, send_ref, p_ref):
    width = 2 * slots * rank
    lane = lax.broadcasted_iota(jnp.int32, (rank, width), 1)
    row = lax.broadcasted_iota(jnp.int32, (rank, width), 0)
    spread = (lane % rank == row).astype(jnp.bfloat16)
    tiled = jnp.dot(c_ref[...], spread, preferred_element_type=jnp.float32)
    lane = lax.broadcasted_iota(jnp.int32, (slots * tokens, width), 1)
    row = lax.broadcasted_iota(jnp.int32, (slots * tokens, width), 0)
    own = (lane // rank) % slots == row // tokens
    blocks = jnp.where(own, tiled, 0.0).astype(jnp.bfloat16)
    p_ref[...] = lax.dot_general(
        a_ref[...], blocks, (((0,), (0,)), ((), ())), preferred_element_type=jnp.float32
    )
    half = chunk // 2
    left = lax.broadcasted_iota(jnp.int32, (half, width), 1) < slots * rank
    groups = keep_ref.shape[0] // half

    def pack(core, out_ref):
        for i in range(groups):
            start = (CORES * i + core) * chunk
            out_ref[pl.ds(half * i, half), :] = jnp.where(
                left, p_ref[pl.ds(start, half), :], p_ref[pl.ds(start + half, half), :]
            )

    core = place[2]

    @pl.when(core == 0)
    def _():
        pack(1, send_ref)
        pack(0, keep_ref)

    @pl.when(core == 1)
    def _():
        pack(0, send_ref)
        pack(1, keep_ref)


def pair_send_kernel(place, keep_ref, got_ref, send_ref):
    rows = send_ref.shape[0]
    there = pl.ds(pl.multiple_of((1 - place[1]) * rows, 8), rows)
    send_ref[...] = keep_ref[there, :] + got_ref[there, :]


def ring_send_kernel(place, keep_ref, got_ref, pair_ref, ring_ref):
    rows = pair_ref.shape[0]
    here = pl.ds(pl.multiple_of(place[1] * rows, 8), rows)
    total = keep_ref[here, :] + got_ref[here, :] + pair_ref[...]
    count, _, width = ring_ref.shape
    half = rows // count
    blank = jnp.zeros((PAD_ROWS - half, width), jnp.float32)
    for i in range(count):
        ring_ref[i, pl.ds(0, half), :] = total[i * half : (i + 1) * half, :]
        ring_ref[i, pl.ds(half, PAD_ROWS - half), :] = blank


def route_kernel(slots, rank, place, counts, ring_ref, out_ref):
    owners, rows, _ = out_ref.shape
    width = ring_ref.shape[2]
    section = place[0]
    offset = jnp.int32(0)
    for s in range(owners):
        offset = offset + jnp.where(s < section, counts[s], 0)
    live = counts[section]
    total = jnp.sum(ring_ref[...], axis=0)
    lane = lax.broadcasted_iota(jnp.int32, (rows, width), 1)
    total = jnp.where((lane // rank) % slots < live, total, 0.0)
    square = jnp.sum(total * total)
    last = lax.broadcasted_iota(jnp.int32, (rows, 2 * LANES), 0) == rows - 1
    out_ref[...] = jnp.broadcast_to(jnp.where(last, square, 0.0)[None], out_ref.shape)
    side = lax.broadcasted_iota(jnp.int32, (rows, LANES), 1) // rank
    depths = owners * DEPTHS_PER_OWNER
    for k in range(slots):
        depth = lax.rem(offset + k + depths // 2, depths)
        owner = depth // DEPTHS_PER_OWNER
        spot = depth - owner * DEPTHS_PER_OWNER

        @pl.when(k < live)
        def _():
            for h in range(2):
                block = h * slots + k
                tile = total[:, (block // 2) * LANES : (block // 2 + 1) * LANES]
                turned = pltpu.roll(tile, rank, 1)
                value = jnp.where(side == block % 2, tile, 0.0)
                moved = jnp.where(side != block % 2, turned, 0.0)
                at = (owner, slice(None), pl.ds(h * LANES, LANES))
                out_ref[at] = out_ref[at] + jnp.where(spot == block % 2, value, moved)


def own_kernel(got_ref, owned_ref, square_ref):
    total = jnp.sum(got_ref[...], axis=0)
    owned_ref[...] = total
    square_ref[...] = jnp.broadcast_to(total[total.shape[0] - 1 :, :LANES], square_ref.shape)


def clip_kernel(entries, rank, owned_ref, squares_ref, out_ref):
    total = jnp.sum(squares_ref[...], axis=0)
    factor = jnp.minimum(1.0, 0.5 / jnp.sqrt(total / entries + 1e-06))
    half = out_ref.shape[1] // 2
    factor = jnp.broadcast_to(factor[:1, :], (half, LANES))
    for h in range(2):
        tile = owned_ref[pl.ds(0, half), pl.ds(h * LANES, LANES)] * factor
        turned = pltpu.roll(owned_ref[:, pl.ds(h * LANES, LANES)], rank, 1)[:half] * factor
        out_ref[0, pl.ds(half * h, half), :] = tile[:, :rank]
        out_ref[1, pl.ds(half * h, half), :] = turned[:, :rank]


def on_device(counts, activations, cotangents):
    _, slots, tokens, hidden = activations.shape
    rank = cotangents.shape[3]
    sections, ring = lax.axis_size("section"), lax.axis_size("ring")
    chunk = hidden // (Y_PAIR * ring * CORES)
    width = 2 * slots * rank
    half = chunk // 2
    place = jnp.stack(
        [lax.axis_index("section"), lax.axis_index("pair"), lax.axis_index("core")]
    ).astype(jnp.int32)
    rows = Y_PAIR * ring * half
    swap = [(0, 1), (1, 0)]
    with jax.named_scope("partials"):
        keep, send = call(
            functools.partial(partial_kernel, slots, tokens, rank, chunk),
            [(rows, width)] * 2,
            [SMEM, VMEM, VMEM],
            [pltpu.VMEM((hidden, width), jnp.float32)],
        )(
            place,
            activations.reshape(slots * tokens, hidden),
            cotangents.reshape(slots * tokens, rank),
        )
    with jax.named_scope("core_sum"):
        got = lax.ppermute(send, "core", swap)
    with jax.named_scope("pair_sum"):
        (send,) = call(pair_send_kernel, [(rows // 2, width)], [SMEM, VMEM, VMEM])(place, keep, got)
        pair = lax.ppermute(send, "pair", swap)
    with jax.named_scope("ring_sum"):
        (blocks,) = call(ring_send_kernel, [(ring, PAD_ROWS, width)], [SMEM, VMEM, VMEM, VMEM])(
            place, keep, got, pair
        )
        blocks = lax.all_to_all(blocks, "ring", 0, 0, tiled=True)
    with jax.named_scope("route"):
        (routed,) = call(
            functools.partial(route_kernel, slots, rank),
            [(sections, PAD_ROWS, 2 * LANES)],
            [SMEM, SMEM, VMEM],
        )(place, counts, blocks)
        routed = lax.all_to_all(routed, "section", 0, 0, tiled=True)
        owned, square = call(own_kernel, [(PAD_ROWS, 2 * LANES), (8, LANES)], [VMEM])(routed)
    with jax.named_scope("norm"):
        square = lax.psum(square, "core")
        squares = jnp.broadcast_to(square[None], (Y_PAIR * ring, 8, LANES))
        squares = lax.all_to_all(squares, ("pair", "ring"), 0, 0, tiled=True)
    with jax.named_scope("clip"):
        entries = sections * DEPTHS_PER_OWNER * hidden * rank
        (out,) = call(
            functools.partial(clip_kernel, entries, rank),
            [(DEPTHS_PER_OWNER, chunk, rank)],
            [VMEM, VMEM],
        )(owned, squares)
    return out


def solution(mesh):
    sections, replicas = mesh.devices.shape
    split = Mesh(
        mesh.devices.reshape(sections, Y_PAIR, replicas // (Y_PAIR * CORES), CORES),
        ("section", "pair", "ring", "core"),
    )
    dp = ("pair", "ring", "core")
    return jax.shard_map(
        on_device,
        mesh=split,
        in_specs=(P(), P("section", None, dp, None), P("section", None, dp, None)),
        out_specs=P("section", dp, None),
        check_vma=False,
    )
```

```python
import functools

import jax
import jax.numpy as jnp
from jax import lax
from jax.experimental import pallas as pl
from jax.experimental.pallas import tpu as pltpu
from jax.sharding import Mesh, PartitionSpec as P

DEPTHS_PER_OWNER = 2
Y_PAIR = 2
NEAR = 2
CORES = 2
LANES = 128
PAD_ROWS = 16
VMEM = pl.BlockSpec(memory_space=pltpu.VMEM)
SMEM = pl.BlockSpec(memory_space=pltpu.SMEM)


def call(body, shapes, in_specs, scratch=()):
    return pl.pallas_call(
        body,
        out_shape=tuple(jax.ShapeDtypeStruct(s, jnp.float32) for s in shapes),
        in_specs=in_specs,
        out_specs=tuple(VMEM for _ in shapes),
        scratch_shapes=list(scratch),
        compiler_params=pltpu.CompilerParams(vmem_limit_bytes=24 * 1024 * 1024),
    )


def partial_kernel(chunk, far, place, a_ref, c_ref, keep_ref, send_ref, p_ref):
    slots, rank, tokens = c_ref.shape
    width = 2 * slots * rank
    lane = lax.broadcasted_iota(jnp.int32, (rank, width), 1)
    row = lax.broadcasted_iota(jnp.int32, (rank, width), 0)
    spread = (lane % rank == row).astype(jnp.bfloat16)
    slot = (lax.broadcasted_iota(jnp.int32, (tokens, width), 1) // rank) % slots
    over_rows = (((0,), (0,)), ((), ()))
    blocks = []
    for k in range(slots):
        tiled = lax.dot_general(c_ref[k], spread, over_rows, preferred_element_type=jnp.float32)
        blocks.append(jnp.where(slot == k, tiled, 0.0).astype(jnp.bfloat16))
    p_ref[...] = lax.dot_general(
        a_ref[...],
        jnp.concatenate(blocks, axis=0),
        over_rows,
        preferred_element_type=jnp.float32,
    )
    half = chunk // 2
    left = lax.broadcasted_iota(jnp.int32, (half, width), 1) < slots * rank

    def pack(core, out_ref):
        at = 0
        for pair in range(Y_PAIR):
            for near in range(NEAR):
                for step in range(far):
                    start = (((pair * far + step) * NEAR + near) * CORES + core) * chunk
                    out_ref[pl.ds(at, half), :] = jnp.where(
                        left, p_ref[pl.ds(start, half), :], p_ref[pl.ds(start + half, half), :]
                    )
                    at += half

    core = place[1]

    @pl.when(core == 0)
    def _():
        pack(1, send_ref)
        pack(0, keep_ref)

    @pl.when(core == 1)
    def _():
        pack(0, send_ref)
        pack(1, keep_ref)


def core_sum_kernel(keep_ref, got_ref, out_ref):
    groups, rows, _ = out_ref.shape
    for i in range(groups):
        at = pl.ds(i * rows, rows)
        out_ref[i] = keep_ref[at, :] + got_ref[at, :]


def near_sum_kernel(got_ref, out_ref):
    total = jnp.sum(got_ref[...], axis=0)
    far = out_ref.shape[0]
    half, tiles = total.shape[0] // far, total.shape[1] // LANES
    for i in range(far):
        for r in range(half):
            for t in range(tiles):
                piece = total[i * half + r : i * half + r + 1, t * LANES : (t + 1) * LANES]
                out_ref[i, :, pl.ds((r * tiles + t) * LANES, LANES)] = piece


def route_kernel(slots, rank, place, counts, got_ref, out_ref, total_ref):
    owners, rows, _ = out_ref.shape
    width = total_ref.shape[1]
    tiles = width // LANES
    half = got_ref.shape[2] // width
    section = place[0]
    offset = jnp.int32(0)
    for s in range(owners):
        offset = offset + jnp.where(s < section, counts[s], 0)
    live = counts[section]
    flat = jnp.sum(got_ref[...], axis=0)
    total_ref[...] = jnp.zeros_like(total_ref)
    for r in range(half):
        for t in range(tiles):
            at = (r * tiles + t) * LANES
            total_ref[pl.ds(r, 1), pl.ds(t * LANES, LANES)] = flat[:, at : at + LANES]
    lane = lax.broadcasted_iota(jnp.int32, (rows, width), 1)
    total = jnp.where((lane // rank) % slots < live, total_ref[...], 0.0)
    square = jnp.sum(total * total)
    last = lax.broadcasted_iota(jnp.int32, (rows, 2 * LANES), 0) == rows - 1
    out_ref[...] = jnp.broadcast_to(jnp.where(last, square, 0.0)[None], out_ref.shape)
    side = lax.broadcasted_iota(jnp.int32, (rows, LANES), 1) // rank
    depths = owners * DEPTHS_PER_OWNER
    for k in range(slots):
        depth = lax.rem(offset + k + depths // 2, depths)
        owner = depth // DEPTHS_PER_OWNER
        spot = depth - owner * DEPTHS_PER_OWNER

        @pl.when(k < live)
        def _():
            for h in range(2):
                block = h * slots + k
                tile = total[:, (block // 2) * LANES : (block // 2 + 1) * LANES]
                turned = pltpu.roll(tile, rank, 1)
                value = jnp.where(side == block % 2, tile, 0.0)
                moved = jnp.where(side != block % 2, turned, 0.0)
                at = (owner, slice(None), pl.ds(h * LANES, LANES))
                out_ref[at] = out_ref[at] + jnp.where(spot == block % 2, value, moved)


def own_kernel(got_ref, owned_ref, square_ref):
    total = jnp.sum(got_ref[...], axis=0)
    owned_ref[...] = total
    square = total[total.shape[0] - 1 :, :LANES]
    square_ref[...] = jnp.broadcast_to(square[None], square_ref.shape)


def clip_kernel(entries, owned_ref, squares_ref, out_ref):
    chunk, _, rank = out_ref.shape
    half = chunk // 2
    total = jnp.sum(squares_ref[...], axis=0)
    factor = jnp.minimum(1.0, 0.5 / jnp.sqrt(total / entries + 1e-06))
    factor = jnp.broadcast_to(factor, (half, LANES))
    for h in range(2):
        tile = owned_ref[pl.ds(0, half), pl.ds(h * LANES, LANES)] * factor
        turned = pltpu.roll(owned_ref[:, pl.ds(h * LANES, LANES)], rank, 1)[:half] * factor
        out_ref[pl.ds(half * h, half), 0, :] = tile[:, :rank]
        out_ref[pl.ds(half * h, half), 1, :] = turned[:, :rank]


def on_device(counts, activations, cotangents):
    _, slots, tokens, hidden = activations.shape
    rank = cotangents.shape[3]
    sections, far = lax.axis_size("section"), lax.axis_size("far")
    replicas = Y_PAIR * far * NEAR * CORES
    chunk = hidden // replicas
    width = 2 * slots * rank
    half = chunk // 2
    place = jnp.stack([lax.axis_index("section"), lax.axis_index("core")]).astype(jnp.int32)
    groups = Y_PAIR * NEAR
    rows = groups * far * half
    with jax.named_scope("partials"):
        keep, send = call(
            functools.partial(partial_kernel, chunk, far),
            [(rows, width)] * 2,
            [SMEM, VMEM, VMEM],
            [pltpu.VMEM((hidden, width), jnp.float32)],
        )(
            place,
            activations.reshape(slots * tokens, hidden),
            jnp.swapaxes(cotangents[0], 1, 2),
        )
    with jax.named_scope("core_sum"):
        got = lax.ppermute(send, "core", [(0, 1), (1, 0)])
        (blocks,) = call(core_sum_kernel, [(groups, far * half, width)], [VMEM] * 2)(keep, got)
    with jax.named_scope("near_sum"):
        blocks = lax.all_to_all(blocks, ("pair", "near"), 0, 0, tiled=True)
        (blocks,) = call(near_sum_kernel, [(far, 1, half * width)], [VMEM])(blocks)
    with jax.named_scope("far_sum"):
        blocks = lax.all_to_all(blocks, "far", 0, 0, tiled=True)
    with jax.named_scope("route"):
        (routed,) = call(
            functools.partial(route_kernel, slots, rank),
            [(sections, PAD_ROWS, 2 * LANES)],
            [SMEM, SMEM, VMEM],
            [pltpu.VMEM((PAD_ROWS, width), jnp.float32)],
        )(place, counts, blocks)
        routed = lax.all_to_all(routed, "section", 0, 0, tiled=True)
        owned, squares = call(
            own_kernel, [(PAD_ROWS, 2 * LANES), (replicas, 1, LANES)], [VMEM]
        )(routed)
    with jax.named_scope("norm"):
        squares = lax.all_to_all(squares, ("pair", "far", "near", "core"), 0, 0, tiled=True)
    with jax.named_scope("clip"):
        entries = sections * DEPTHS_PER_OWNER * hidden * rank
        (out,) = call(
            functools.partial(clip_kernel, entries),
            [(chunk, DEPTHS_PER_OWNER, rank)],
            [VMEM, VMEM],
        )(owned, squares)
    return jnp.swapaxes(out, 0, 1)


def solution(mesh):
    sections, replicas = mesh.devices.shape
    far = replicas // (Y_PAIR * NEAR * CORES)
    split = Mesh(
        mesh.devices.reshape(sections, Y_PAIR, far, NEAR, CORES),
        ("section", "pair", "far", "near", "core"),
    )
    dp = ("pair", "far", "near", "core")
    return jax.shard_map(
        on_device,
        mesh=split,
        in_specs=(P(), P("section", None, dp, None), P("section", None, dp, None)),
        out_specs=P("section", dp, None),
        check_vma=False,
    )
```

```python
import functools

import jax
import jax.numpy as jnp
from jax import lax
from jax.experimental import pallas as pl
from jax.experimental.pallas import tpu as pltpu
from jax.sharding import Mesh, PartitionSpec as P

DEPTHS_PER_OWNER = 2
Y_PAIR = 2
NEAR = 2
CORES = 2
LANES = 128
PAD_ROWS = 16
TILES = 3
OVER_ROWS = (((0,), (0,)), ((), ()))
VMEM = pl.BlockSpec(memory_space=pltpu.VMEM)
SMEM = pl.BlockSpec(memory_space=pltpu.SMEM)


def call(body, shapes, in_specs, scratch=(), dtype=jnp.float32, cost=None):
    return pl.pallas_call(
        body,
        out_shape=tuple(jax.ShapeDtypeStruct(s, dtype) for s in shapes),
        in_specs=in_specs,
        out_specs=tuple(VMEM for _ in shapes),
        scratch_shapes=list(scratch),
        cost_estimate=cost,
        compiler_params=pltpu.CompilerParams(vmem_limit_bytes=24 * 1024 * 1024),
    )


def spread_kernel(c_ref, blocks_ref):
    slots, rank, tokens = c_ref.shape
    width = blocks_ref.shape[1]
    lane = lax.broadcasted_iota(jnp.int32, (rank, width), 1)
    row = lax.broadcasted_iota(jnp.int32, (rank, width), 0)
    spread = (lane % rank == row).astype(jnp.bfloat16)
    slot = jnp.minimum(lax.broadcasted_iota(jnp.int32, (tokens, width), 1) // rank, slots - 1)
    for k in range(slots):
        tiled = lax.dot_general(c_ref[k], spread, OVER_ROWS, preferred_element_type=jnp.float32)
        blocks_ref[pl.ds(k * tokens, tokens), :] = jnp.where(slot == k, tiled, 0.0).astype(jnp.bfloat16)


def partial_kernel(chunk, far, a_ref, blocks_ref, keep_ref, send_ref, p_ref):
    sums = lax.dot_general(a_ref[...], blocks_ref[...], OVER_ROWS, preferred_element_type=jnp.float32)
    for t in range(2):
        p_ref[t] = sums[:, t * LANES : (t + 1) * LANES]
    half = chunk // 2
    left = lax.broadcasted_iota(jnp.int32, (half, LANES), 1) < LANES // 2

    def pack(core, out_ref):
        for pair in range(Y_PAIR):
            for near in range(NEAR):
                for step in range(far):
                    start = (((pair * far + step) * NEAR + near) * CORES + core) * chunk
                    upper, lower = pl.ds(start, half), pl.ds(start + half, half)
                    tiles = (
                        p_ref[0, upper, :],
                        jnp.where(left, p_ref[1, upper, :], p_ref[1, lower, :]),
                        p_ref[0, lower, :],
                    )
                    for t in range(TILES):
                        at = pl.ds((t * far + step) * half, half)
                        out_ref[pair * NEAR + near, at, :] = tiles[t]

    core = lax.axis_index("core")

    @pl.when(core == 0)
    def _():
        pack(1, send_ref)
        pack(0, keep_ref)

    @pl.when(core == 1)
    def _():
        pack(0, send_ref)
        pack(1, keep_ref)


def core_sum_kernel(mask_ref, keep_ref, got_ref, out_ref):
    del mask_ref
    out_ref[...] = keep_ref[...] + got_ref[...]


def near_sum_kernel(got_ref, out_ref):
    total = jnp.sum(got_ref[...], axis=0)
    far = out_ref.shape[0]
    half = total.shape[0] // (TILES * far)
    for i in range(far):
        for t in range(TILES):
            for r in range(half):
                row = (t * far + i) * half + r
                out_ref[i, :, pl.ds((t * half + r) * LANES, LANES)] = total[row : row + 1, :]


def mask_kernel(slots, rank, counts, mask_ref):
    owners = counts.shape[0]
    section = lax.axis_index("section")
    offset = jnp.int32(0)
    for s in range(owners):
        offset = offset + jnp.where(s < section, counts[s], 0)
    live = counts[section]
    row = lax.broadcasted_iota(jnp.int32, mask_ref.shape, 0)
    side = lax.broadcasted_iota(jnp.int32, mask_ref.shape, 1) // rank
    depths = owners * DEPTHS_PER_OWNER
    mask = jnp.zeros(mask_ref.shape, jnp.bool_)
    for k in range(slots):
        depth = lax.rem(offset + k + depths // 2, depths)
        owner = depth // DEPTHS_PER_OWNER
        spot = depth - owner * DEPTHS_PER_OWNER
        mask = mask | ((row == owner * slots + k) & (side == spot) & (k < live))
    base = owners * slots
    mask = mask | ((row == base) & (side < live)) | ((row == base + 1) & (slots - 1 < live))
    mask_ref[...] = mask.astype(jnp.float32)


def route_kernel(slots, mask_ref, got_ref, out_ref, total_ref):
    owners, rows, _ = out_ref.shape
    half = got_ref.shape[2] // (TILES * LANES)
    flat = jnp.sum(got_ref[...], axis=0)
    total_ref[...] = jnp.zeros_like(total_ref)
    for t in range(TILES):
        for r in range(half):
            at = (t * half + r) * LANES
            total_ref[t, pl.ds(r, 1), :] = flat[:, at : at + LANES]
    base = owners * slots
    first, last = mask_ref[pl.ds(base, 1), :], mask_ref[pl.ds(base + 1, 1), :]
    live = (first, last, first)
    tiles = [total_ref[t] * live[t] for t in range(TILES)]
    squares = jnp.sum(sum(x * x for x in tiles), axis=0, keepdims=True)
    left = lax.broadcasted_iota(jnp.int32, (rows, LANES), 1) < LANES // 2
    turned = [pltpu.roll(x, LANES // 2, 1) for x in tiles]
    both = [jnp.where(left, x, y) for x, y in zip(tiles, turned)]
    flip = [jnp.where(left, y, x) for x, y in zip(tiles, turned)]
    halves = ((both[0], flip[0], both[1]), (both[2], flip[2], flip[1]))
    bottom = lax.broadcasted_iota(jnp.int32, (rows, LANES), 0) == rows - 1
    blank = jnp.where(bottom, squares, 0.0)
    for e in range(owners):
        for h in range(2):
            value = blank
            for k in range(slots):
                value = value + mask_ref[pl.ds(e * slots + k, 1), :] * halves[h][k]
            out_ref[e, :, pl.ds(h * LANES, LANES)] = value


def own_kernel(got_ref, owned_ref, square_ref):
    total = jnp.sum(got_ref[...], axis=0)
    owned_ref[...] = total
    square = total[total.shape[0] - 1 :, :LANES]
    square_ref[...] = jnp.broadcast_to(square[None], square_ref.shape)


def clip_kernel(entries, owned_ref, squares_ref, out_ref):
    chunk, _, rank = out_ref.shape
    half = chunk // 2
    total = jnp.sum(jnp.sum(squares_ref[...], axis=0), axis=1, keepdims=True)
    factor = jnp.minimum(1.0, 0.5 / jnp.sqrt(total / entries + 1e-06))
    factor = jnp.broadcast_to(factor, (half, LANES))
    for h in range(2):
        tile = owned_ref[pl.ds(0, half), pl.ds(h * LANES, LANES)] * factor
        turned = pltpu.roll(owned_ref[:, pl.ds(h * LANES, LANES)], rank, 1)[:half] * factor
        out_ref[pl.ds(half * h, half), 0, :] = tile[:, :rank]
        out_ref[pl.ds(half * h, half), 1, :] = turned[:, :rank]


def on_device(counts, activations, cotangents):
    _, slots, tokens, hidden = activations.shape
    rank = cotangents.shape[3]
    sections, far = lax.axis_size("section"), lax.axis_size("far")
    replicas = Y_PAIR * far * NEAR * CORES
    chunk = hidden // replicas
    half = chunk // 2
    groups = Y_PAIR * NEAR
    packed = (groups, TILES * far * half, LANES)
    with jax.named_scope("partials"):
        (blocks,) = call(
            spread_kernel,
            [(slots * tokens, 2 * LANES)],
            [VMEM],
            dtype=jnp.bfloat16,
            cost=pl.CostEstimate(flops=4 * 10**9, bytes_accessed=10**6, transcendentals=0),
        )(jnp.swapaxes(cotangents[0], 1, 2))
        keep, send = call(
            functools.partial(partial_kernel, chunk, far),
            [packed] * 2,
            [VMEM, VMEM],
            [pltpu.VMEM((2, hidden, LANES), jnp.float32)],
        )(activations.reshape(slots * tokens, hidden), blocks)
    with jax.named_scope("core_sum"):
        got = lax.ppermute(send, "core", [(0, 1), (1, 0)])
        (mask,) = call(
            functools.partial(mask_kernel, slots, rank), [(sections * slots + 8, LANES)], [SMEM]
        )(counts)
        (blocks,) = call(core_sum_kernel, [packed], [VMEM] * 3)(mask, keep, got)
    with jax.named_scope("near_sum"):
        blocks = lax.all_to_all(blocks, ("pair", "near"), 0, 0, tiled=True)
        (blocks,) = call(near_sum_kernel, [(far, 1, TILES * half * LANES)], [VMEM])(blocks)
    with jax.named_scope("far_sum"):
        blocks = lax.all_to_all(blocks, "far", 0, 0, tiled=True)
    with jax.named_scope("route"):
        (routed,) = call(
            functools.partial(route_kernel, slots),
            [(sections, PAD_ROWS, 2 * LANES)],
            [VMEM, VMEM],
            [pltpu.VMEM((TILES, PAD_ROWS, LANES), jnp.float32)],
        )(mask, blocks)
        routed = lax.all_to_all(routed, "section", 0, 0, tiled=True)
        owned, squares = call(
            own_kernel, [(PAD_ROWS, 2 * LANES), (replicas, 1, LANES)], [VMEM]
        )(routed)
    with jax.named_scope("norm"):
        squares = lax.all_to_all(squares, ("pair", "far", "near", "core"), 0, 0, tiled=True)
    with jax.named_scope("clip"):
        entries = sections * DEPTHS_PER_OWNER * hidden * rank
        (out,) = call(
            functools.partial(clip_kernel, entries),
            [(chunk, DEPTHS_PER_OWNER, rank)],
            [VMEM, VMEM],
        )(owned, squares)
    return jnp.swapaxes(out, 0, 1)


def solution(mesh):
    sections, replicas = mesh.devices.shape
    far = replicas // (Y_PAIR * NEAR * CORES)
    split = Mesh(
        mesh.devices.reshape(sections, Y_PAIR, far, NEAR, CORES),
        ("section", "pair", "far", "near", "core"),
    )
    dp = ("pair", "far", "near", "core")
    return jax.shard_map(
        on_device,
        mesh=split,
        in_specs=(P(), P("section", None, dp, None), P("section", None, dp, None)),
        out_specs=P("section", dp, None),
        check_vma=False,
    )
```

```python
import functools

import jax
import jax.numpy as jnp
from jax import lax
from jax.experimental import pallas as pl
from jax.experimental.pallas import tpu as pltpu
from jax.sharding import Mesh, PartitionSpec as P

DEPTHS_PER_OWNER = 2
Y_PAIR = 2
NEAR = 2
CORES = 2
LANES = 128
PAD_ROWS = 16
TILES = 3
OVER_ROWS = (((0,), (0,)), ((), ()))
VMEM = pl.BlockSpec(memory_space=pltpu.VMEM)
SMEM = pl.BlockSpec(memory_space=pltpu.SMEM)


def call(body, shapes, in_specs, scratch=(), dtype=jnp.float32, cost=None):
    return pl.pallas_call(
        body,
        out_shape=tuple(jax.ShapeDtypeStruct(s, dtype) for s in shapes),
        in_specs=in_specs,
        out_specs=tuple(VMEM for _ in shapes),
        scratch_shapes=list(scratch),
        cost_estimate=cost,
        compiler_params=pltpu.CompilerParams(vmem_limit_bytes=24 * 1024 * 1024),
    )


def spread_kernel(spread_ref):
    rank, width = spread_ref.shape
    lane = lax.broadcasted_iota(jnp.int32, (rank, width), 1)
    row = lax.broadcasted_iota(jnp.int32, (rank, width), 0)
    spread_ref[...] = (lane % rank == row).astype(jnp.bfloat16)


def blocks_kernel(spread_ref, c_ref, blocks_ref):
    slots, rank, tokens = c_ref.shape
    width = blocks_ref.shape[1]
    slot = jnp.minimum(lax.broadcasted_iota(jnp.int32, (tokens, width), 1) // rank, slots - 1)
    for k in range(slots):
        tiled = lax.dot_general(
            c_ref[k], spread_ref[...], OVER_ROWS, preferred_element_type=jnp.float32
        )
        blocks_ref[pl.ds(k * tokens, tokens), :] = jnp.where(slot == k, tiled, 0.0).astype(jnp.bfloat16)


def partial_kernel(chunk, far, a_ref, blocks_ref, keep_ref, send_ref, p_ref):
    sums = lax.dot_general(a_ref[...], blocks_ref[...], OVER_ROWS, preferred_element_type=jnp.float32)
    for t in range(2):
        p_ref[t] = sums[:, t * LANES : (t + 1) * LANES]
    half = chunk // 2
    left = lax.broadcasted_iota(jnp.int32, (half, LANES), 1) < LANES // 2

    def pack(core, out_ref):
        for pair in range(Y_PAIR):
            for near in range(NEAR):
                for step in range(far):
                    start = (((pair * far + step) * NEAR + near) * CORES + core) * chunk
                    upper, lower = pl.ds(start, half), pl.ds(start + half, half)
                    tiles = (
                        p_ref[0, upper, :],
                        jnp.where(left, p_ref[1, upper, :], p_ref[1, lower, :]),
                        p_ref[0, lower, :],
                    )
                    for t in range(TILES):
                        at = pl.ds((t * far + step) * half, half)
                        out_ref[pair * NEAR + near, at, :] = tiles[t]

    core = lax.axis_index("core")

    @pl.when(core == 0)
    def _():
        pack(1, send_ref)
        pack(0, keep_ref)

    @pl.when(core == 1)
    def _():
        pack(0, send_ref)
        pack(1, keep_ref)


def core_sum_kernel(mask_ref, keep_ref, got_ref, out_ref):
    del mask_ref
    out_ref[...] = keep_ref[...] + got_ref[...]


def near_sum_kernel(order, got_ref, out_ref):
    total = jnp.sum(got_ref[...], axis=0)
    far = out_ref.shape[0]
    half = total.shape[0] // (TILES * far)
    for i in range(far):
        for t in range(TILES):
            for r in range(half):
                row = (t * far + order[i]) * half + r
                out_ref[i, :, pl.ds((t * half + r) * LANES, LANES)] = total[row : row + 1, :]


def mask_kernel(slots, rank, counts, mask_ref):
    owners = counts.shape[0]
    section = lax.axis_index("section")
    offset = jnp.int32(0)
    for s in range(owners):
        offset = offset + jnp.where(s < section, counts[s], 0)
    live = counts[section]
    row = lax.broadcasted_iota(jnp.int32, mask_ref.shape, 0)
    side = lax.broadcasted_iota(jnp.int32, mask_ref.shape, 1) // rank
    depths = owners * DEPTHS_PER_OWNER
    mask = jnp.zeros(mask_ref.shape, jnp.bool_)
    for k in range(slots):
        depth = lax.rem(offset + k + depths // 2, depths)
        owner = depth // DEPTHS_PER_OWNER
        spot = depth - owner * DEPTHS_PER_OWNER
        mask = mask | ((row == owner * slots + k) & (side == spot) & (k < live))
    base = owners * slots
    mask = mask | ((row == base) & (side < live)) | ((row == base + 1) & (slots - 1 < live))
    mask_ref[...] = mask.astype(jnp.float32)


def route_kernel(slots, mask_ref, got_ref, out_ref, total_ref):
    owners, rows, _ = out_ref.shape
    half = got_ref.shape[2] // (TILES * LANES)
    flat = jnp.sum(got_ref[...], axis=0)
    total_ref[...] = jnp.zeros_like(total_ref)
    for t in range(TILES):
        for r in range(half):
            at = (t * half + r) * LANES
            total_ref[t, pl.ds(r, 1), :] = flat[:, at : at + LANES]
    base = owners * slots
    first, last = mask_ref[pl.ds(base, 1), :], mask_ref[pl.ds(base + 1, 1), :]
    live = (first, last, first)
    tiles = [total_ref[t] * live[t] for t in range(TILES)]
    squares = jnp.sum(sum(x * x for x in tiles), axis=0, keepdims=True)
    left = lax.broadcasted_iota(jnp.int32, (rows, LANES), 1) < LANES // 2
    turned = [pltpu.roll(x, LANES // 2, 1) for x in tiles]
    both = [jnp.where(left, x, y) for x, y in zip(tiles, turned)]
    flip = [jnp.where(left, y, x) for x, y in zip(tiles, turned)]
    halves = ((both[0], flip[0], both[1]), (both[2], flip[2], flip[1]))
    bottom = lax.broadcasted_iota(jnp.int32, (rows, LANES), 0) == rows - 1
    blank = jnp.where(bottom, squares, 0.0)
    for e in range(owners):
        for h in range(2):
            value = blank
            for k in range(slots):
                value = value + mask_ref[pl.ds(e * slots + k, 1), :] * halves[h][k]
            out_ref[e, :, pl.ds(h * LANES, LANES)] = value


def own_kernel(got_ref, owned_ref, square_ref):
    total = jnp.sum(got_ref[...], axis=0)
    owned_ref[...] = total
    square = total[total.shape[0] - 1 :, :LANES]
    square_ref[...] = jnp.broadcast_to(square[None], square_ref.shape)


def clip_kernel(entries, owned_ref, squares_ref, out_ref):
    chunk, _, rank = out_ref.shape
    half = chunk // 2
    total = jnp.sum(jnp.sum(squares_ref[...], axis=0), axis=1, keepdims=True)
    factor = jnp.minimum(1.0, 0.5 / jnp.sqrt(total / entries + 1e-06))
    factor = jnp.broadcast_to(factor, (half, LANES))
    for h in range(2):
        tile = owned_ref[pl.ds(0, half), pl.ds(h * LANES, LANES)] * factor
        turned = pltpu.roll(owned_ref[:, pl.ds(h * LANES, LANES)], rank, 1)[:half] * factor
        out_ref[pl.ds(half * h, half), 0, :] = tile[:, :rank]
        out_ref[pl.ds(half * h, half), 1, :] = turned[:, :rank]


def on_device(counts, activations, cotangents):
    _, slots, tokens, hidden = activations.shape
    rank = cotangents.shape[3]
    sections, far = lax.axis_size("section"), lax.axis_size("far")
    replicas = Y_PAIR * far * NEAR * CORES
    chunk = hidden // replicas
    half = chunk // 2
    groups = Y_PAIR * NEAR
    order = sorted(range(far), key=lambda i: (i % 2, i % (far // 2)))
    packed = (groups, TILES * far * half, LANES)
    with jax.named_scope("partials"):
        hint = pl.CostEstimate(flops=4 * 10**9, bytes_accessed=10**6, transcendentals=0)
        (spread,) = call(spread_kernel, [(rank, 2 * LANES)], [], dtype=jnp.bfloat16, cost=hint)()
        (blocks,) = call(
            blocks_kernel,
            [(slots * tokens, 2 * LANES)],
            [VMEM, VMEM],
            dtype=jnp.bfloat16,
        )(spread, jnp.swapaxes(cotangents[0], 1, 2))
        keep, send = call(
            functools.partial(partial_kernel, chunk, far),
            [packed] * 2,
            [VMEM, VMEM],
            [pltpu.VMEM((2, hidden, LANES), jnp.float32)],
        )(activations.reshape(slots * tokens, hidden), blocks)
    with jax.named_scope("core_sum"):
        got = lax.ppermute(send, "core", [(0, 1), (1, 0)])
        (mask,) = call(
            functools.partial(mask_kernel, slots, rank), [(sections * slots + 8, LANES)], [SMEM]
        )(counts)
        (blocks,) = call(core_sum_kernel, [packed], [VMEM] * 3)(mask, keep, got)
    with jax.named_scope("near_sum"):
        blocks = lax.all_to_all(blocks, ("pair", "near"), 0, 0, tiled=True)
        (blocks,) = call(
            functools.partial(near_sum_kernel, order), [(far, 1, TILES * half * LANES)], [VMEM]
        )(blocks)
    with jax.named_scope("far_sum"):
        blocks = lax.all_to_all(
            blocks, "far", 0, 0, axis_index_groups=[order], tiled=True
        )
    with jax.named_scope("route"):
        (routed,) = call(
            functools.partial(route_kernel, slots),
            [(sections, PAD_ROWS, 2 * LANES)],
            [VMEM, VMEM],
            [pltpu.VMEM((TILES, PAD_ROWS, LANES), jnp.float32)],
        )(mask, blocks)
        routed = lax.all_to_all(routed, "section", 0, 0, tiled=True)
        owned, squares = call(
            own_kernel, [(PAD_ROWS, 2 * LANES), (replicas, 1, LANES)], [VMEM]
        )(routed)
    with jax.named_scope("norm"):
        squares = lax.all_to_all(squares, ("pair", "far", "near", "core"), 0, 0, tiled=True)
    with jax.named_scope("clip"):
        entries = sections * DEPTHS_PER_OWNER * hidden * rank
        (out,) = call(
            functools.partial(clip_kernel, entries),
            [(chunk, DEPTHS_PER_OWNER, rank)],
            [VMEM, VMEM],
        )(owned, squares)
    return jnp.swapaxes(out, 0, 1)


def solution(mesh):
    sections, replicas = mesh.devices.shape
    far = replicas // (Y_PAIR * NEAR * CORES)
    split = Mesh(
        mesh.devices.reshape(sections, Y_PAIR, far, NEAR, CORES),
        ("section", "pair", "far", "near", "core"),
    )
    dp = ("pair", "far", "near", "core")
    return jax.shard_map(
        on_device,
        mesh=split,
        in_specs=(P(), P("section", None, dp, None), P("section", None, dp, None)),
        out_specs=P("section", dp, None),
        check_vma=False,
    )
```

```python
import functools

import jax
import jax.numpy as jnp
from jax import lax
from jax.experimental import pallas as pl
from jax.experimental.pallas import tpu as pltpu
from jax.sharding import Mesh, PartitionSpec as P

DEPTHS_PER_OWNER = 2
Y_PAIR = 2
NEAR = 2
CORES = 2
LANES = 128
PAD_ROWS = 16
TILES = 3
OVER_ROWS = (((0,), (0,)), ((), ()))
VMEM = pl.BlockSpec(memory_space=pltpu.VMEM)
SMEM = pl.BlockSpec(memory_space=pltpu.SMEM)


def call(body, shapes, in_specs, scratch=(), dtype=jnp.float32, cost=None):
    return pl.pallas_call(
        body,
        out_shape=tuple(jax.ShapeDtypeStruct(s, dtype) for s in shapes),
        in_specs=in_specs,
        out_specs=tuple(VMEM for _ in shapes),
        scratch_shapes=list(scratch),
        cost_estimate=cost,
        compiler_params=pltpu.CompilerParams(vmem_limit_bytes=24 * 1024 * 1024),
    )


def spread_kernel(spread_ref):
    rank, width = spread_ref.shape
    lane = lax.broadcasted_iota(jnp.int32, (rank, width), 1)
    row = lax.broadcasted_iota(jnp.int32, (rank, width), 0)
    spread_ref[...] = (lane % rank == row).astype(jnp.bfloat16)


def blocks_kernel(spread_ref, c_ref, blocks_ref):
    slots, rank, tokens = c_ref.shape
    width = blocks_ref.shape[1]
    slot = jnp.minimum(lax.broadcasted_iota(jnp.int32, (tokens, width), 1) // rank, slots - 1)
    for k in range(slots):
        tiled = lax.dot_general(
            c_ref[k], spread_ref[...], OVER_ROWS, preferred_element_type=jnp.float32
        )
        blocks_ref[pl.ds(k * tokens, tokens), :] = jnp.where(slot == k, tiled, 0.0).astype(jnp.bfloat16)


def partial_kernel(chunk, far, a_ref, blocks_ref, keep_ref, send_ref, p_ref):
    sums = lax.dot_general(a_ref[...], blocks_ref[...], OVER_ROWS, preferred_element_type=jnp.float32)
    for t in range(2):
        p_ref[t] = sums[:, t * LANES : (t + 1) * LANES]
    half = chunk // 2
    left = lax.broadcasted_iota(jnp.int32, (half, LANES), 1) < LANES // 2

    def pack(core, out_ref):
        for pair in range(Y_PAIR):
            for near in range(NEAR):
                for step in range(far):
                    start = (((pair * far + step) * NEAR + near) * CORES + core) * chunk
                    upper, lower = pl.ds(start, half), pl.ds(start + half, half)
                    tiles = (
                        p_ref[0, upper, :],
                        jnp.where(left, p_ref[1, upper, :], p_ref[1, lower, :]),
                        p_ref[0, lower, :],
                    )
                    for t in range(TILES):
                        at = pl.ds((t * far + step) * half, half)
                        out_ref[near * Y_PAIR + pair, at, :] = tiles[t]

    core = lax.axis_index("core")

    @pl.when(core == 0)
    def _():
        pack(1, send_ref)
        pack(0, keep_ref)

    @pl.when(core == 1)
    def _():
        pack(0, send_ref)
        pack(1, keep_ref)


def core_sum_kernel(mask_ref, keep_ref, got_ref, out_ref):
    del mask_ref
    out_ref[...] = keep_ref[...] + got_ref[...]


def near_sum_kernel(got_ref, out_ref):
    total = jnp.sum(got_ref[...], axis=0)
    far = out_ref.shape[0]
    half = total.shape[0] // (TILES * far)
    for i in range(far):
        for t in range(TILES):
            for r in range(half):
                row = (t * far + i) * half + r
                out_ref[i, :, pl.ds((t * half + r) * LANES, LANES)] = total[row : row + 1, :]


def mask_kernel(slots, rank, counts, mask_ref):
    owners = counts.shape[0]
    section = lax.axis_index("section")
    offset = jnp.int32(0)
    for s in range(owners):
        offset = offset + jnp.where(s < section, counts[s], 0)
    live = counts[section]
    row = lax.broadcasted_iota(jnp.int32, mask_ref.shape, 0)
    side = lax.broadcasted_iota(jnp.int32, mask_ref.shape, 1) // rank
    depths = owners * DEPTHS_PER_OWNER
    mask = jnp.zeros(mask_ref.shape, jnp.bool_)
    for k in range(slots):
        depth = lax.rem(offset + k + depths // 2, depths)
        owner = depth // DEPTHS_PER_OWNER
        spot = depth - owner * DEPTHS_PER_OWNER
        mask = mask | ((row == owner * slots + k) & (side == spot) & (k < live))
    base = owners * slots
    mask = mask | ((row == base) & (side < live)) | ((row == base + 1) & (slots - 1 < live))
    mask_ref[...] = mask.astype(jnp.float32)


def square_kernel(base, mask_ref, got_ref, total_ref, square_ref):
    half = got_ref.shape[2] // (TILES * LANES)
    flat = jnp.sum(got_ref[...], axis=0)
    total_ref[...] = jnp.zeros_like(total_ref)
    for t in range(TILES):
        for r in range(half):
            at = (t * half + r) * LANES
            total_ref[t, pl.ds(r, 1), :] = flat[:, at : at + LANES]
    first, last = mask_ref[pl.ds(base, 1), :], mask_ref[pl.ds(base + 1, 1), :]
    live = (first, last, first)
    squares = jnp.zeros((total_ref.shape[1], LANES), jnp.float32)
    for t in range(TILES):
        x = total_ref[t] * live[t]
        squares = squares + x * x
    squares = jnp.sum(squares, axis=0, keepdims=True)
    square_ref[...] = jnp.broadcast_to(squares[None], square_ref.shape)


def route_kernel(slots, mask_ref, total_ref, squares_ref, out_ref):
    owners, rows, _ = out_ref.shape
    base = owners * slots
    first, last = mask_ref[pl.ds(base, 1), :], mask_ref[pl.ds(base + 1, 1), :]
    live = (first, last, first)
    tiles = [total_ref[t] * live[t] for t in range(TILES)]
    squares = jnp.sum(squares_ref[...], axis=0)
    left = lax.broadcasted_iota(jnp.int32, (rows, LANES), 1) < LANES // 2
    turned = [pltpu.roll(x, LANES // 2, 1) for x in tiles]
    both = [jnp.where(left, x, y) for x, y in zip(tiles, turned)]
    flip = [jnp.where(left, y, x) for x, y in zip(tiles, turned)]
    halves = ((both[0], flip[0], both[1]), (both[2], flip[2], flip[1]))
    bottom = lax.broadcasted_iota(jnp.int32, (rows, LANES), 0) == rows - 1
    blank = jnp.where(bottom, squares, 0.0)
    for e in range(owners):
        for h in range(2):
            value = blank
            for k in range(slots):
                value = value + mask_ref[pl.ds(e * slots + k, 1), :] * halves[h][k]
            out_ref[e, :, pl.ds(h * LANES, LANES)] = value


def clip_kernel(entries, got_ref, out_ref):
    chunk, _, rank = out_ref.shape
    half = chunk // 2
    owned = jnp.sum(got_ref[...], axis=0)
    square = jnp.sum(owned[owned.shape[0] - 1 :, :LANES], axis=1, keepdims=True)
    factor = jnp.minimum(1.0, 0.5 / jnp.sqrt(square / entries + 1e-06))
    owned = owned * jnp.broadcast_to(factor, owned.shape)
    for h in range(2):
        tile = owned[:, h * LANES : (h + 1) * LANES]
        turned = pltpu.roll(tile, rank, 1)
        out_ref[pl.ds(half * h, half), 0, :] = tile[:half, :rank]
        out_ref[pl.ds(half * h, half), 1, :] = turned[:half, :rank]


def on_device(counts, activations, cotangents):
    _, slots, tokens, hidden = activations.shape
    rank = cotangents.shape[3]
    sections, far = lax.axis_size("section"), lax.axis_size("far")
    replicas = Y_PAIR * far * NEAR * CORES
    chunk = hidden // replicas
    half = chunk // 2
    groups = Y_PAIR * NEAR
    packed = (groups, TILES * far * half, LANES)
    with jax.named_scope("partials"):
        hint = pl.CostEstimate(flops=4 * 10**9, bytes_accessed=10**6, transcendentals=0)
        (spread,) = call(spread_kernel, [(rank, 2 * LANES)], [], dtype=jnp.bfloat16, cost=hint)()
        (blocks,) = call(
            blocks_kernel,
            [(slots * tokens, 2 * LANES)],
            [VMEM, VMEM],
            dtype=jnp.bfloat16,
        )(spread, jnp.swapaxes(cotangents[0], 1, 2))
        keep, send = call(
            functools.partial(partial_kernel, chunk, far),
            [packed] * 2,
            [VMEM, VMEM],
            [pltpu.VMEM((2, hidden, LANES), jnp.float32)],
        )(activations.reshape(slots * tokens, hidden), blocks)
    with jax.named_scope("core_sum"):
        got = lax.ppermute(send, "core", [(0, 1), (1, 0)])
        (mask,) = call(
            functools.partial(mask_kernel, slots, rank), [(sections * slots + 8, LANES)], [SMEM]
        )(counts)
        (blocks,) = call(core_sum_kernel, [packed], [VMEM] * 3)(mask, keep, got)
    with jax.named_scope("near_sum"):
        blocks = lax.all_to_all(blocks, ("near", "pair"), 0, 0, tiled=True)
        (blocks,) = call(near_sum_kernel, [(far, 1, TILES * half * LANES)], [VMEM])(blocks)
    with jax.named_scope("far_sum"):
        blocks = lax.all_to_all(blocks, "far", 0, 0, tiled=True)
    with jax.named_scope("norm"):
        total, squares = call(
            functools.partial(square_kernel, sections * slots),
            [(TILES, PAD_ROWS, LANES), (replicas, 1, LANES)],
            [VMEM, VMEM],
        )(mask, blocks)
        squares = lax.all_to_all(squares, ("pair", "far", "near", "core"), 0, 0, tiled=True)
    with jax.named_scope("route"):
        (routed,) = call(
            functools.partial(route_kernel, slots),
            [(sections, PAD_ROWS, 2 * LANES)],
            [VMEM] * 3,
        )(mask, total, squares)
        routed = lax.all_to_all(routed, "section", 0, 0, tiled=True)
    with jax.named_scope("clip"):
        entries = sections * DEPTHS_PER_OWNER * hidden * rank
        (out,) = call(
            functools.partial(clip_kernel, entries),
            [(chunk, DEPTHS_PER_OWNER, rank)],
            [VMEM],
        )(routed)
    return jnp.swapaxes(out, 0, 1)


def solution(mesh):
    sections, replicas = mesh.devices.shape
    far = replicas // (Y_PAIR * NEAR * CORES)
    split = Mesh(
        mesh.devices.reshape(sections, Y_PAIR, far, NEAR, CORES),
        ("section", "pair", "far", "near", "core"),
    )
    dp = ("pair", "far", "near", "core")
    return jax.shard_map(
        on_device,
        mesh=split,
        in_specs=(P(), P("section", None, dp, None), P("section", None, dp, None)),
        out_specs=P("section", dp, None),
        check_vma=False,
    )
```

```python
import functools

import jax
import jax.numpy as jnp
from jax import lax
from jax.experimental import pallas as pl
from jax.experimental.pallas import tpu as pltpu
from jax.sharding import Mesh, PartitionSpec as P

DEPTHS_PER_OWNER = 2
Y_PAIR = 2
NEAR = 2
CORES = 2
LANES = 128
PAD_ROWS = 16
TILES = 3
OVER_ROWS = (((0,), (0,)), ((), ()))
VMEM = pl.BlockSpec(memory_space=pltpu.VMEM)
SMEM = pl.BlockSpec(memory_space=pltpu.SMEM)


def call(body, shapes, in_specs, scratch=(), dtype=jnp.float32, cost=None):
    return pl.pallas_call(
        body,
        out_shape=tuple(jax.ShapeDtypeStruct(s, dtype) for s in shapes),
        in_specs=in_specs,
        out_specs=tuple(VMEM for _ in shapes),
        scratch_shapes=list(scratch),
        cost_estimate=cost,
        compiler_params=pltpu.CompilerParams(vmem_limit_bytes=24 * 1024 * 1024),
    )


def spread_kernel(spread_ref):
    rank, width = spread_ref.shape
    lane = lax.broadcasted_iota(jnp.int32, (rank, width), 1)
    row = lax.broadcasted_iota(jnp.int32, (rank, width), 0)
    spread_ref[...] = (lane % rank == row).astype(jnp.bfloat16)


def blocks_kernel(spread_ref, c_ref, blocks_ref):
    slots, rank, tokens = c_ref.shape
    width = blocks_ref.shape[1]
    slot = jnp.minimum(lax.broadcasted_iota(jnp.int32, (tokens, width), 1) // rank, slots - 1)
    for k in range(slots):
        tiled = lax.dot_general(
            c_ref[k], spread_ref[...], OVER_ROWS, preferred_element_type=jnp.float32
        )
        blocks_ref[pl.ds(k * tokens, tokens), :] = jnp.where(slot == k, tiled, 0.0).astype(jnp.bfloat16)


def partial_kernel(chunk, far, a_ref, blocks_ref, keep_ref, send_ref, p_ref):
    sums = lax.dot_general(a_ref[...], blocks_ref[...], OVER_ROWS, preferred_element_type=jnp.float32)
    for t in range(2):
        p_ref[t] = sums[:, t * LANES : (t + 1) * LANES]
    half = chunk // 2
    left = lax.broadcasted_iota(jnp.int32, (half, LANES), 1) < LANES // 2

    def pack(core, out_ref):
        for pair in range(Y_PAIR):
            for near in range(NEAR):
                for step in range(far):
                    start = (((pair * far + step) * NEAR + near) * CORES + core) * chunk
                    upper, lower = pl.ds(start, half), pl.ds(start + half, half)
                    tiles = (
                        p_ref[0, upper, :],
                        jnp.where(left, p_ref[1, upper, :], p_ref[1, lower, :]),
                        p_ref[0, lower, :],
                    )
                    for t in range(TILES):
                        at = pl.ds((t * far + step) * half, half)
                        out_ref[near * Y_PAIR + pair, at, :] = tiles[t]

    core = lax.axis_index("core")

    @pl.when(core == 0)
    def _():
        pack(1, send_ref)
        pack(0, keep_ref)

    @pl.when(core == 1)
    def _():
        pack(0, send_ref)
        pack(1, keep_ref)


def core_sum_kernel(mask_ref, keep_ref, got_ref, out_ref):
    del mask_ref
    out_ref[...] = keep_ref[...] + got_ref[...]


def near_sum_kernel(order, got_ref, out_ref):
    total = jnp.sum(got_ref[...], axis=0)
    far = out_ref.shape[0]
    half = total.shape[0] // (TILES * far)
    for i in range(far):
        for t in range(TILES):
            for r in range(half):
                row = (t * far + order[i]) * half + r
                out_ref[i, :, pl.ds((t * half + r) * LANES, LANES)] = total[row : row + 1, :]


def mask_kernel(slots, rank, counts, mask_ref):
    owners = counts.shape[0]
    section = lax.axis_index("section")
    offset = jnp.int32(0)
    for s in range(owners):
        offset = offset + jnp.where(s < section, counts[s], 0)
    live = counts[section]
    row = lax.broadcasted_iota(jnp.int32, mask_ref.shape, 0)
    side = lax.broadcasted_iota(jnp.int32, mask_ref.shape, 1) // rank
    depths = owners * DEPTHS_PER_OWNER
    mask = jnp.zeros(mask_ref.shape, jnp.bool_)
    for k in range(slots):
        depth = lax.rem(offset + k + depths // 2, depths)
        owner = depth // DEPTHS_PER_OWNER
        spot = depth - owner * DEPTHS_PER_OWNER
        mask = mask | ((row == owner * slots + k) & (side == spot) & (k < live))
    base = owners * slots
    mask = mask | ((row == base) & (side < live)) | ((row == base + 1) & (slots - 1 < live))
    mask_ref[...] = mask.astype(jnp.float32)


def square_kernel(base, mask_ref, got_ref, total_ref, square_ref):
    half = got_ref.shape[2] // (TILES * LANES)
    flat = jnp.sum(got_ref[...], axis=0)
    total_ref[...] = jnp.zeros_like(total_ref)
    for t in range(TILES):
        for r in range(half):
            at = (t * half + r) * LANES
            total_ref[t, pl.ds(r, 1), :] = flat[:, at : at + LANES]
    first, last = mask_ref[pl.ds(base, 1), :], mask_ref[pl.ds(base + 1, 1), :]
    live = (first, last, first)
    squares = jnp.zeros((total_ref.shape[1], LANES), jnp.float32)
    for t in range(TILES):
        x = total_ref[t] * live[t]
        squares = squares + x * x
    squares = jnp.sum(squares, axis=0, keepdims=True)
    square_ref[...] = jnp.broadcast_to(squares[None], square_ref.shape)


def route_kernel(slots, mask_ref, total_ref, squares_ref, out_ref):
    owners, rows, _ = out_ref.shape
    base = owners * slots
    first, last = mask_ref[pl.ds(base, 1), :], mask_ref[pl.ds(base + 1, 1), :]
    live = (first, last, first)
    tiles = [total_ref[t] * live[t] for t in range(TILES)]
    squares = jnp.sum(squares_ref[...], axis=0)
    left = lax.broadcasted_iota(jnp.int32, (rows, LANES), 1) < LANES // 2
    turned = [pltpu.roll(x, LANES // 2, 1) for x in tiles]
    both = [jnp.where(left, x, y) for x, y in zip(tiles, turned)]
    flip = [jnp.where(left, y, x) for x, y in zip(tiles, turned)]
    halves = ((both[0], flip[0], both[1]), (both[2], flip[2], flip[1]))
    bottom = lax.broadcasted_iota(jnp.int32, (rows, LANES), 0) == rows - 1
    blank = jnp.where(bottom, squares, 0.0)
    for e in range(owners):
        for h in range(2):
            value = blank
            for k in range(slots):
                value = value + mask_ref[pl.ds(e * slots + k, 1), :] * halves[h][k]
            out_ref[e, :, pl.ds(h * LANES, LANES)] = value


def clip_kernel(entries, got_ref, out_ref):
    chunk, _, rank = out_ref.shape
    half = chunk // 2
    owned = jnp.sum(got_ref[...], axis=0)
    square = jnp.sum(owned[owned.shape[0] - 1 :, :LANES], axis=1, keepdims=True)
    factor = jnp.minimum(1.0, 0.5 / jnp.sqrt(square / entries + 1e-06))
    owned = owned * jnp.broadcast_to(factor, owned.shape)
    for h in range(2):
        tile = owned[:, h * LANES : (h + 1) * LANES]
        turned = pltpu.roll(tile, rank, 1)
        out_ref[pl.ds(half * h, half), 0, :] = tile[:half, :rank]
        out_ref[pl.ds(half * h, half), 1, :] = turned[:half, :rank]


def on_device(counts, activations, cotangents):
    _, slots, tokens, hidden = activations.shape
    rank = cotangents.shape[3]
    sections, far = lax.axis_size("section"), lax.axis_size("far")
    replicas = Y_PAIR * far * NEAR * CORES
    chunk = hidden // replicas
    half = chunk // 2
    groups = Y_PAIR * NEAR
    order = sorted(range(far), key=lambda i: (i * (far // 2 - 1)) % far)
    packed = (groups, TILES * far * half, LANES)
    with jax.named_scope("partials"):
        hint = pl.CostEstimate(flops=4 * 10**9, bytes_accessed=10**6, transcendentals=0)
        (spread,) = call(spread_kernel, [(rank, 2 * LANES)], [], dtype=jnp.bfloat16, cost=hint)()
        (blocks,) = call(
            blocks_kernel,
            [(slots * tokens, 2 * LANES)],
            [VMEM, VMEM],
            dtype=jnp.bfloat16,
        )(spread, jnp.swapaxes(cotangents[0], 1, 2))
        keep, send = call(
            functools.partial(partial_kernel, chunk, far),
            [packed] * 2,
            [VMEM, VMEM],
            [pltpu.VMEM((2, hidden, LANES), jnp.float32)],
        )(activations.reshape(slots * tokens, hidden), blocks)
    with jax.named_scope("core_sum"):
        got = lax.ppermute(send, "core", [(0, 1), (1, 0)])
        (mask,) = call(
            functools.partial(mask_kernel, slots, rank), [(sections * slots + 8, LANES)], [SMEM]
        )(counts)
        (blocks,) = call(core_sum_kernel, [packed], [VMEM] * 3)(mask, keep, got)
    with jax.named_scope("near_sum"):
        blocks = lax.all_to_all(blocks, ("near", "pair"), 0, 0, tiled=True)
        (blocks,) = call(
            functools.partial(near_sum_kernel, order), [(far, 1, TILES * half * LANES)], [VMEM]
        )(blocks)
    with jax.named_scope("far_sum"):
        blocks = lax.all_to_all(
            blocks, "far", 0, 0, axis_index_groups=[order], tiled=True
        )
    with jax.named_scope("norm"):
        total, squares = call(
            functools.partial(square_kernel, sections * slots),
            [(TILES, PAD_ROWS, LANES), (replicas, 1, LANES)],
            [VMEM, VMEM],
        )(mask, blocks)
        squares = lax.all_to_all(squares, ("pair", "far", "near", "core"), 0, 0, tiled=True)
    with jax.named_scope("route"):
        (routed,) = call(
            functools.partial(route_kernel, slots),
            [(sections, PAD_ROWS, 2 * LANES)],
            [VMEM] * 3,
        )(mask, total, squares)
        routed = lax.all_to_all(routed, "section", 0, 0, tiled=True)
    with jax.named_scope("clip"):
        entries = sections * DEPTHS_PER_OWNER * hidden * rank
        (out,) = call(
            functools.partial(clip_kernel, entries),
            [(chunk, DEPTHS_PER_OWNER, rank)],
            [VMEM],
        )(routed)
    return jnp.swapaxes(out, 0, 1)


def solution(mesh):
    sections, replicas = mesh.devices.shape
    far = replicas // (Y_PAIR * NEAR * CORES)
    split = Mesh(
        mesh.devices.reshape(sections, Y_PAIR, far, NEAR, CORES),
        ("section", "pair", "far", "near", "core"),
    )
    dp = ("pair", "far", "near", "core")
    return jax.shard_map(
        on_device,
        mesh=split,
        in_specs=(P(), P("section", None, dp, None), P("section", None, dp, None)),
        out_specs=P("section", dp, None),
        check_vma=False,
    )
```

```python
import functools

import jax
import jax.numpy as jnp
from jax import lax
from jax.experimental import pallas as pl
from jax.experimental.pallas import tpu as pltpu
from jax.sharding import Mesh, PartitionSpec as P

DEPTHS_PER_OWNER = 2
Y_PAIR = 2
NEAR = 2
CORES = 2
LANES = 128
PAD_ROWS = 16
TILES = 3
OVER_ROWS = (((0,), (0,)), ((), ()))
VMEM = pl.BlockSpec(memory_space=pltpu.VMEM)
SMEM = pl.BlockSpec(memory_space=pltpu.SMEM)


def call(body, shapes, in_specs, scratch=(), dtype=jnp.float32, cost=None):
    return pl.pallas_call(
        body,
        out_shape=tuple(jax.ShapeDtypeStruct(s, dtype) for s in shapes),
        in_specs=in_specs,
        out_specs=tuple(VMEM for _ in shapes),
        scratch_shapes=list(scratch),
        cost_estimate=cost,
        compiler_params=pltpu.CompilerParams(vmem_limit_bytes=24 * 1024 * 1024),
    )


def spread_kernel(spread_ref):
    rank, width = spread_ref.shape
    lane = lax.broadcasted_iota(jnp.int32, (rank, width), 1)
    row = lax.broadcasted_iota(jnp.int32, (rank, width), 0)
    spread_ref[...] = (lane % rank == row).astype(jnp.bfloat16)


def blocks_kernel(spread_ref, c_ref, blocks_ref):
    slots, rank, tokens = c_ref.shape
    width = blocks_ref.shape[1]
    slot = jnp.minimum(lax.broadcasted_iota(jnp.int32, (tokens, width), 1) // rank, slots - 1)
    for k in range(slots):
        tiled = lax.dot_general(
            c_ref[k], spread_ref[...], OVER_ROWS, preferred_element_type=jnp.float32
        )
        blocks_ref[pl.ds(k * tokens, tokens), :] = jnp.where(slot == k, tiled, 0.0).astype(jnp.bfloat16)


def partial_kernel(chunk, far, a_ref, blocks_ref, keep_ref, send_ref, p_ref):
    sums = lax.dot_general(a_ref[...], blocks_ref[...], OVER_ROWS, preferred_element_type=jnp.float32)
    for t in range(2):
        p_ref[t] = sums[:, t * LANES : (t + 1) * LANES]
    half = chunk // 2
    left = lax.broadcasted_iota(jnp.int32, (half, LANES), 1) < LANES // 2

    def pack(core, out_ref):
        for pair in range(Y_PAIR):
            for near in range(NEAR):
                for step in range(far):
                    start = (((pair * far + step) * NEAR + near) * CORES + core) * chunk
                    upper, lower = pl.ds(start, half), pl.ds(start + half, half)
                    tiles = (
                        p_ref[0, upper, :],
                        jnp.where(left, p_ref[1, upper, :], p_ref[1, lower, :]),
                        p_ref[0, lower, :],
                    )
                    for t in range(TILES):
                        at = pl.ds((t * far + step) * half, half)
                        out_ref[near * Y_PAIR + pair, at, :] = tiles[t]

    core = lax.axis_index("core")

    @pl.when(core == 0)
    def _():
        pack(1, send_ref)
        pack(0, keep_ref)

    @pl.when(core == 1)
    def _():
        pack(0, send_ref)
        pack(1, keep_ref)


def core_sum_kernel(mask_ref, keep_ref, got_ref, out_ref):
    del mask_ref
    out_ref[...] = keep_ref[...] + got_ref[...]


def near_sum_kernel(order, got_ref, out_ref):
    total = jnp.sum(got_ref[...], axis=0)
    far = out_ref.shape[0]
    half = total.shape[0] // (TILES * far)
    for i in range(far):
        for t in range(TILES):
            for r in range(half):
                row = (t * far + order[i]) * half + r
                out_ref[i, :, pl.ds((t * half + r) * LANES, LANES)] = total[row : row + 1, :]


def mask_kernel(slots, rank, counts, mask_ref):
    owners = counts.shape[0]
    section = lax.axis_index("section")
    offset = jnp.int32(0)
    for s in range(owners):
        offset = offset + jnp.where(s < section, counts[s], 0)
    live = counts[section]
    row = lax.broadcasted_iota(jnp.int32, mask_ref.shape, 0)
    side = lax.broadcasted_iota(jnp.int32, mask_ref.shape, 1) // rank
    depths = owners * DEPTHS_PER_OWNER
    mask = jnp.zeros(mask_ref.shape, jnp.bool_)
    for k in range(slots):
        depth = lax.rem(offset + k + depths // 2, depths)
        owner = depth // DEPTHS_PER_OWNER
        spot = depth - owner * DEPTHS_PER_OWNER
        mask = mask | ((row == owner * slots + k) & (side == spot) & (k < live))
    base = owners * slots
    mask = mask | ((row == base) & (side < live)) | ((row == base + 1) & (slots - 1 < live))
    mask_ref[...] = mask.astype(jnp.float32)


def square_kernel(base, mask_ref, got_ref, total_ref, square_ref):
    half = got_ref.shape[2] // (TILES * LANES)
    flat = jnp.sum(got_ref[...], axis=0)
    total_ref[...] = jnp.zeros_like(total_ref)
    for t in range(TILES):
        for r in range(half):
            at = (t * half + r) * LANES
            total_ref[t, pl.ds(r, 1), :] = flat[:, at : at + LANES]
    first, last = mask_ref[pl.ds(base, 1), :], mask_ref[pl.ds(base + 1, 1), :]
    live = (first, last, first)
    squares = jnp.zeros((total_ref.shape[1], LANES), jnp.float32)
    for t in range(TILES):
        x = total_ref[t] * live[t]
        squares = squares + x * x
    squares = jnp.sum(squares, axis=0, keepdims=True)
    square_ref[...] = jnp.broadcast_to(squares[None], square_ref.shape)


def route_kernel(slots, mask_ref, total_ref, squares_ref, out_ref):
    owners, _, size = out_ref.shape
    _, rows, _ = total_ref.shape
    half = (size // LANES - 1) // 2
    base = owners * slots
    first, last = mask_ref[pl.ds(base, 1), :], mask_ref[pl.ds(base + 1, 1), :]
    live = (first, last, first)
    tiles = [total_ref[t] * live[t] for t in range(TILES)]
    squares = jnp.sum(squares_ref[...], axis=0)
    left = lax.broadcasted_iota(jnp.int32, (rows, LANES), 1) < LANES // 2
    turned = [pltpu.roll(x, LANES // 2, 1) for x in tiles]
    both = [jnp.where(left, x, y) for x, y in zip(tiles, turned)]
    flip = [jnp.where(left, y, x) for x, y in zip(tiles, turned)]
    halves = ((both[0], flip[0], both[1]), (both[2], flip[2], flip[1]))
    for e in range(owners):
        for h in range(2):
            value = jnp.zeros((rows, LANES), jnp.float32)
            for k in range(slots):
                value = value + mask_ref[pl.ds(e * slots + k, 1), :] * halves[h][k]
            for r in range(half):
                out_ref[e, :, pl.ds((h * half + r) * LANES, LANES)] = value[r : r + 1, :]
        out_ref[e, :, pl.ds(2 * half * LANES, LANES)] = squares


def clip_kernel(entries, got_ref, out_ref, owned_ref):
    chunk, _, rank = out_ref.shape
    half = chunk // 2
    flat = jnp.sum(got_ref[...], axis=0)
    owned_ref[...] = jnp.zeros_like(owned_ref)
    for h in range(2):
        for r in range(half):
            at = (h * half + r) * LANES
            owned_ref[h, pl.ds(r, 1), :] = flat[:, at : at + LANES]
    square = jnp.sum(flat[:, chunk * LANES :], axis=1, keepdims=True)
    factor = jnp.minimum(1.0, 0.5 / jnp.sqrt(square / entries + 1e-06))
    factor = jnp.broadcast_to(factor, owned_ref.shape[1:])
    for h in range(2):
        tile = owned_ref[h] * factor
        turned = pltpu.roll(tile, rank, 1)
        out_ref[pl.ds(half * h, half), 0, :] = tile[:half, :rank]
        out_ref[pl.ds(half * h, half), 1, :] = turned[:half, :rank]


def on_device(counts, activations, cotangents):
    _, slots, tokens, hidden = activations.shape
    rank = cotangents.shape[3]
    sections, far = lax.axis_size("section"), lax.axis_size("far")
    replicas = Y_PAIR * far * NEAR * CORES
    chunk = hidden // replicas
    half = chunk // 2
    groups = Y_PAIR * NEAR
    order = sorted(range(far), key=lambda i: (i * (far // 2 - 1)) % far)
    packed = (groups, TILES * far * half, LANES)
    with jax.named_scope("partials"):
        hint = pl.CostEstimate(flops=4 * 10**9, bytes_accessed=10**6, transcendentals=0)
        (spread,) = call(spread_kernel, [(rank, 2 * LANES)], [], dtype=jnp.bfloat16, cost=hint)()
        (blocks,) = call(
            blocks_kernel,
            [(slots * tokens, 2 * LANES)],
            [VMEM, VMEM],
            dtype=jnp.bfloat16,
        )(spread, jnp.swapaxes(cotangents[0], 1, 2))
        keep, send = call(
            functools.partial(partial_kernel, chunk, far),
            [packed] * 2,
            [VMEM, VMEM],
            [pltpu.VMEM((2, hidden, LANES), jnp.float32)],
        )(activations.reshape(slots * tokens, hidden), blocks)
    with jax.named_scope("core_sum"):
        got = lax.ppermute(send, "core", [(0, 1), (1, 0)])
        (mask,) = call(
            functools.partial(mask_kernel, slots, rank), [(sections * slots + 8, LANES)], [SMEM]
        )(counts)
        (blocks,) = call(core_sum_kernel, [packed], [VMEM] * 3)(mask, keep, got)
    with jax.named_scope("near_sum"):
        blocks = lax.all_to_all(blocks, ("near", "pair"), 0, 0, tiled=True)
        (blocks,) = call(
            functools.partial(near_sum_kernel, order), [(far, 1, TILES * half * LANES)], [VMEM]
        )(blocks)
    with jax.named_scope("far_sum"):
        blocks = lax.all_to_all(
            blocks, "far", 0, 0, axis_index_groups=[order], tiled=True
        )
    with jax.named_scope("norm"):
        total, squares = call(
            functools.partial(square_kernel, sections * slots),
            [(TILES, PAD_ROWS, LANES), (replicas, 1, LANES)],
            [VMEM, VMEM],
        )(mask, blocks)
        squares = lax.all_to_all(squares, ("pair", "far", "near", "core"), 0, 0, tiled=True)
    with jax.named_scope("route"):
        (routed,) = call(
            functools.partial(route_kernel, slots),
            [(sections, 1, (chunk + 1) * LANES)],
            [VMEM] * 3,
        )(mask, total, squares)
        routed = lax.all_to_all(routed, "section", 0, 0, tiled=True)
    with jax.named_scope("clip"):
        entries = sections * DEPTHS_PER_OWNER * hidden * rank
        (out,) = call(
            functools.partial(clip_kernel, entries),
            [(chunk, DEPTHS_PER_OWNER, rank)],
            [VMEM],
            [pltpu.VMEM((2, PAD_ROWS, LANES), jnp.float32)],
        )(routed)
    return jnp.swapaxes(out, 0, 1)


def solution(mesh):
    sections, replicas = mesh.devices.shape
    far = replicas // (Y_PAIR * NEAR * CORES)
    split = Mesh(
        mesh.devices.reshape(sections, Y_PAIR, far, NEAR, CORES),
        ("section", "pair", "far", "near", "core"),
    )
    dp = ("pair", "far", "near", "core")
    return jax.shard_map(
        on_device,
        mesh=split,
        in_specs=(P(), P("section", None, dp, None), P("section", None, dp, None)),
        out_specs=P("section", dp, None),
        check_vma=False,
    )
```

```python
import functools

import jax
import jax.numpy as jnp
from jax import lax
from jax.experimental import pallas as pl
from jax.experimental.pallas import tpu as pltpu
from jax.sharding import Mesh, PartitionSpec as P

DEPTHS_PER_OWNER = 2
Y_PAIR = 2
NEAR = 2
CORES = 2
LANES = 128
PAD_ROWS = 16
TILES = 3
OVER_ROWS = (((0,), (0,)), ((), ()))
VMEM = pl.BlockSpec(memory_space=pltpu.VMEM)
SMEM = pl.BlockSpec(memory_space=pltpu.SMEM)


def call(body, shapes, in_specs, scratch=(), dtype=jnp.float32, cost=None):
    return pl.pallas_call(
        body,
        out_shape=tuple(jax.ShapeDtypeStruct(s, dtype) for s in shapes),
        in_specs=in_specs,
        out_specs=tuple(VMEM for _ in shapes),
        scratch_shapes=list(scratch),
        cost_estimate=cost,
        compiler_params=pltpu.CompilerParams(vmem_limit_bytes=24 * 1024 * 1024),
    )


def spread_kernel(spread_ref):
    rank, width = spread_ref.shape
    lane = lax.broadcasted_iota(jnp.int32, (rank, width), 1)
    row = lax.broadcasted_iota(jnp.int32, (rank, width), 0)
    spread_ref[...] = (lane % rank == row).astype(jnp.bfloat16)


def blocks_kernel(spread_ref, c_ref, blocks_ref):
    slots, rank, tokens = c_ref.shape
    width = blocks_ref.shape[1]
    slot = jnp.minimum(lax.broadcasted_iota(jnp.int32, (tokens, width), 1) // rank, slots - 1)
    for k in range(slots):
        tiled = lax.dot_general(
            c_ref[k], spread_ref[...], OVER_ROWS, preferred_element_type=jnp.float32
        )
        blocks_ref[pl.ds(k * tokens, tokens), :] = jnp.where(slot == k, tiled, 0.0).astype(jnp.bfloat16)


def partial_kernel(chunk, far, a_ref, blocks_ref, keep_ref, send_ref, p_ref):
    sums = lax.dot_general(a_ref[...], blocks_ref[...], OVER_ROWS, preferred_element_type=jnp.float32)
    for t in range(2):
        p_ref[t] = sums[:, t * LANES : (t + 1) * LANES]
    half = chunk // 2
    left = lax.broadcasted_iota(jnp.int32, (half, LANES), 1) < LANES // 2

    def pack(core, out_ref):
        for pair in range(Y_PAIR):
            for near in range(NEAR):
                for step in range(far):
                    start = (((pair * far + step) * NEAR + near) * CORES + core) * chunk
                    upper, lower = pl.ds(start, half), pl.ds(start + half, half)
                    tiles = (
                        p_ref[0, upper, :],
                        jnp.where(left, p_ref[1, upper, :], p_ref[1, lower, :]),
                        p_ref[0, lower, :],
                    )
                    for t in range(TILES):
                        at = pl.ds((t * far + step) * half, half)
                        out_ref[near * Y_PAIR + pair, at, :] = tiles[t]

    core = lax.axis_index("core")

    @pl.when(core == 0)
    def _():
        pack(1, send_ref)
        pack(0, keep_ref)

    @pl.when(core == 1)
    def _():
        pack(0, send_ref)
        pack(1, keep_ref)


def core_sum_kernel(mask_ref, keep_ref, got_ref, out_ref):
    del mask_ref
    out_ref[...] = keep_ref[...] + got_ref[...]


def near_sum_kernel(order, got_ref, out_ref):
    total = jnp.sum(got_ref[...], axis=0)
    far = out_ref.shape[0]
    half = total.shape[0] // (TILES * far)
    for i in range(far):
        for t in range(TILES):
            for r in range(half):
                row = (t * far + order[i]) * half + r
                out_ref[i, :, pl.ds((t * half + r) * LANES, LANES)] = total[row : row + 1, :]


def mask_kernel(slots, rank, counts, mask_ref):
    owners = counts.shape[0]
    section = lax.axis_index("section")
    offset = jnp.int32(0)
    for s in range(owners):
        offset = offset + jnp.where(s < section, counts[s], 0)
    live = counts[section]
    row = lax.broadcasted_iota(jnp.int32, mask_ref.shape, 0)
    side = lax.broadcasted_iota(jnp.int32, mask_ref.shape, 1) // rank
    depths = owners * DEPTHS_PER_OWNER
    mask = jnp.zeros(mask_ref.shape, jnp.bool_)
    for k in range(slots):
        depth = lax.rem(offset + k + depths // 2, depths)
        owner = depth // DEPTHS_PER_OWNER
        spot = depth - owner * DEPTHS_PER_OWNER
        mask = mask | ((row == owner * slots + k) & (side == spot) & (k < live))
    base = owners * slots
    mask = mask | ((row == base) & (side < live)) | ((row == base + 1) & (slots - 1 < live))
    mask_ref[...] = mask.astype(jnp.float32)


def square_kernel(base, mask_ref, got_ref, total_ref, square_ref):
    half = got_ref.shape[2] // (TILES * LANES)
    flat = jnp.sum(got_ref[...], axis=0)
    total_ref[...] = jnp.zeros_like(total_ref)
    for t in range(TILES):
        for r in range(half):
            at = (t * half + r) * LANES
            total_ref[t, pl.ds(r, 1), :] = flat[:, at : at + LANES]
    first, last = mask_ref[pl.ds(base, 1), :], mask_ref[pl.ds(base + 1, 1), :]
    live = (first, last, first)
    squares = jnp.zeros((total_ref.shape[1], LANES), jnp.float32)
    for t in range(TILES):
        x = total_ref[t] * live[t]
        squares = squares + x * x
    squares = jnp.sum(squares, axis=0, keepdims=True)
    square_ref[...] = jnp.broadcast_to(squares[None], square_ref.shape)


def route_kernel(slots, mask_ref, total_ref, squares_ref, out_ref):
    owners, _, size = out_ref.shape
    _, rows, _ = total_ref.shape
    half = (size // LANES - 1) // 2
    base = owners * slots
    first, last = mask_ref[pl.ds(base, 1), :], mask_ref[pl.ds(base + 1, 1), :]
    live = (first, last, first)
    tiles = [total_ref[t] * live[t] for t in range(TILES)]
    squares = jnp.sum(squares_ref[...], axis=0)
    left = lax.broadcasted_iota(jnp.int32, (rows, LANES), 1) < LANES // 2
    turned = [pltpu.roll(x, LANES // 2, 1) for x in tiles]
    both = [jnp.where(left, x, y) for x, y in zip(tiles, turned)]
    flip = [jnp.where(left, y, x) for x, y in zip(tiles, turned)]
    halves = ((both[0], flip[0], both[1]), (both[2], flip[2], flip[1]))
    for e in range(owners):
        for h in range(2):
            value = jnp.zeros((rows, LANES), jnp.float32)
            for k in range(slots):
                value = value + mask_ref[pl.ds(e * slots + k, 1), :] * halves[h][k]
            for r in range(half):
                out_ref[e, :, pl.ds((h * half + r) * LANES, LANES)] = value[r : r + 1, :]
        out_ref[e, :, pl.ds(2 * half * LANES, LANES)] = squares


def clip_kernel(entries, got_ref, out_ref, owned_ref):
    chunk, _, rank = out_ref.shape
    half = chunk // 2
    flat = jnp.sum(got_ref[...], axis=0)
    owned_ref[...] = jnp.zeros_like(owned_ref)
    for h in range(2):
        for r in range(half):
            at = (h * half + r) * LANES
            owned_ref[h, pl.ds(r, 1), :] = flat[:, at : at + LANES]
    square = jnp.sum(flat[:, chunk * LANES :], axis=1, keepdims=True)
    factor = jnp.minimum(1.0, 0.5 / jnp.sqrt(square / entries + 1e-06))
    factor = jnp.broadcast_to(factor, owned_ref.shape[1:])
    for h in range(2):
        tile = owned_ref[h] * factor
        turned = pltpu.roll(tile, rank, 1)
        out_ref[pl.ds(half * h, half), 0, :] = tile[:half, :rank]
        out_ref[pl.ds(half * h, half), 1, :] = turned[:half, :rank]


def on_device(counts, activations, cotangents):
    _, slots, tokens, hidden = activations.shape
    rank = cotangents.shape[3]
    sections, far = lax.axis_size("section"), lax.axis_size("far")
    replicas = Y_PAIR * far * NEAR * CORES
    chunk = hidden // replicas
    half = chunk // 2
    groups = Y_PAIR * NEAR
    order = sorted(range(far), key=lambda i: (i * (far // 2 + 1)) % far)
    packed = (groups, TILES * far * half, LANES)
    with jax.named_scope("partials"):
        hint = pl.CostEstimate(flops=4 * 10**9, bytes_accessed=10**6, transcendentals=0)
        (spread,) = call(spread_kernel, [(rank, 2 * LANES)], [], dtype=jnp.bfloat16, cost=hint)()
        (blocks,) = call(
            blocks_kernel,
            [(slots * tokens, 2 * LANES)],
            [VMEM, VMEM],
            dtype=jnp.bfloat16,
        )(spread, jnp.swapaxes(cotangents[0], 1, 2))
        keep, send = call(
            functools.partial(partial_kernel, chunk, far),
            [packed] * 2,
            [VMEM, VMEM],
            [pltpu.VMEM((2, hidden, LANES), jnp.float32)],
        )(activations.reshape(slots * tokens, hidden), blocks)
    with jax.named_scope("core_sum"):
        got = lax.ppermute(send, "core", [(0, 1), (1, 0)])
        (mask,) = call(
            functools.partial(mask_kernel, slots, rank), [(sections * slots + 8, LANES)], [SMEM]
        )(counts)
        (blocks,) = call(core_sum_kernel, [packed], [VMEM] * 3)(mask, keep, got)
    with jax.named_scope("near_sum"):
        blocks = lax.all_to_all(blocks, ("near", "pair"), 0, 0, tiled=True)
        (blocks,) = call(
            functools.partial(near_sum_kernel, order), [(far, 1, TILES * half * LANES)], [VMEM]
        )(blocks)
    with jax.named_scope("far_sum"):
        blocks = lax.all_to_all(
            blocks, "far", 0, 0, axis_index_groups=[order], tiled=True
        )
    with jax.named_scope("norm"):
        total, squares = call(
            functools.partial(square_kernel, sections * slots),
            [(TILES, PAD_ROWS, LANES), (replicas, 1, LANES)],
            [VMEM, VMEM],
        )(mask, blocks)
        squares = lax.all_to_all(squares, ("pair", "far", "near", "core"), 0, 0, tiled=True)
    with jax.named_scope("route"):
        (routed,) = call(
            functools.partial(route_kernel, slots),
            [(sections, 1, (chunk + 1) * LANES)],
            [VMEM] * 3,
        )(mask, total, squares)
        routed = lax.all_to_all(routed, "section", 0, 0, tiled=True)
    with jax.named_scope("clip"):
        entries = sections * DEPTHS_PER_OWNER * hidden * rank
        (out,) = call(
            functools.partial(clip_kernel, entries),
            [(chunk, DEPTHS_PER_OWNER, rank)],
            [VMEM],
            [pltpu.VMEM((2, PAD_ROWS, LANES), jnp.float32)],
        )(routed)
    return jnp.swapaxes(out, 0, 1)


def solution(mesh):
    sections, replicas = mesh.devices.shape
    far = replicas // (Y_PAIR * NEAR * CORES)
    split = Mesh(
        mesh.devices.reshape(sections, Y_PAIR, far, NEAR, CORES),
        ("section", "pair", "far", "near", "core"),
    )
    dp = ("pair", "far", "near", "core")
    return jax.shard_map(
        on_device,
        mesh=split,
        in_specs=(P(), P("section", None, dp, None), P("section", None, dp, None)),
        out_specs=P("section", dp, None),
        check_vma=False,
    )
```
